256 devices in a mesh: blk: 8 (over y, x_hi), head: 32 (over x_lo, z, core).
Axes of the slice: x: 4 (x_hi: 2, x_lo: 2; x = x_hi * 2 + x_lo), y: 4, z: 8, core: 2. Of those that a mesh axis runs over, the one named last changes fastest.
Arguments:
- queries: bfloat16 [32768, 3072], P(('blk', 'head')), may hold values from -150 to 150
- keys_in: bfloat16 [32768, 3072], P(('blk', 'head')), may hold values from -6 to 6
- values: bfloat16 [32768, 3072], P(('blk', 'head')), may hold values from -6 to 6
- out_grad: bfloat16 [32768, 3072], P(('blk', 'head')), may hold values from -6 to 6
- doc_lengths: int32 [32], replicated, may hold values from 1 to 2048, 32768 in all
Outputs:
- query_grad: bfloat16 [32768, 3072], P(('blk', 'head'))
- key_grad: bfloat16 [32768, 3072], P(('blk', 'head'))
- value_grad: bfloat16 [32768, 3072], P(('blk', 'head'))
The draws below stay inside these ranges and needn't reach their ends.
Inputs may be any that keep to these rules, and one draw needn't show every extreme that they name: `doc_lengths`: 32 lengths that sum to 32768; the largest is exactly 2048.
All inputs are finite; a program needn't handle non-finite values.
Results may differ from the reference program's by a relative error of at most 0.0053.
Values may be sent and summed in bfloat16 or wider, within the bound.
No kernel may reach another device: no remote copies, remote signals or barrier semaphores. Data moves between devices by JAX's collectives and lax.ppermute only.
A program may use at most 64 MiB of HBM per device.

```python
import math
import jax
import jax.numpy as jnp
import numpy as np
from jax import lax

H = 32
HD = 96
D = 3072
QBLK = 512
TOKENS = 32768
MAXDOC = 2048
DOCS = 32


def shared_keys(key):
    return jnp.clip(jax.random.normal(jax.random.fold_in(key, 5), (TOKENS, D), jnp.float32), -6.0, 6.0)


def draw_keys_in(key, part):
    return shared_keys(key).astype(jnp.bfloat16)


def draw_queries(key, part):
    key = jax.random.fold_in(key, 3)
    return jnp.clip(jax.random.normal(key, (TOKENS, D), jnp.float32), -6.0, 6.0).astype(jnp.bfloat16)


def level_of(key, dims, shards, low, top_value):
    level, own = 1.0, jax.random.fold_in(key, 6)
    for dim, parts in shards:
        heights = jnp.exp(jax.random.uniform(jax.random.fold_in(own, dim), (parts,), jnp.float32, low / len(shards), top_value / len(shards)))
        level = level * jnp.repeat(heights, dims[dim] // parts).reshape([-1 if axis == dim else 1 for axis in range(len(dims))])
    return level


def split_up(number_of, total, most, skew):
    loads = [(1 << 20) // math.isqrt(standing ** skew) + 1 for standing in range(2, number_of + 1)]
    rest, given = total - most - (number_of - 1), [1] * (number_of - 1)
    while rest > 0:
        candidates = [i for i in range(number_of - 1) if given[i] < most]
        whole, left = sum([loads[i] for i in candidates]), rest
        for i in candidates:
            extra = min(most - given[i], max(1, left * loads[i] // whole), rest)
            given[i] = given[i] + extra
            rest = rest - extra
    return np.array([most] + given)


def ragged(stream_key, amount, total, most, slope):
    if amount == 2:
        one = jax.random.randint(stream_key, (), max(1, total - most), min(most, total - 1) + 1)
        return jnp.stack([one, total - one])
    tallies = jnp.asarray(split_up(amount, total, most, slope), jnp.int32)
    twos = (amount - 1) // 2
    source_of, taker = tallies[1:1 + 2 * twos:2], tallies[2:2 + 2 * twos:2]
    margin = jnp.minimum(source_of - 1, most - taker)
    shifted = jax.random.randint(jax.random.fold_in(stream_key, 1), (twos,), 0, 1 << 20) % (margin + 1)
    tallies = tallies.at[1:1 + 2 * twos:2].set(source_of - shifted).at[2:2 + 2 * twos:2].set(taker + shifted)
    return tallies[jax.random.permutation(jax.random.fold_in(stream_key, 2), amount)]


def gaussian(key, shape, scale, most, pieces=(), kind=jnp.bfloat16):
    gain = level_of(key, shape, pieces, -0.22, 0.18) if pieces else 1.0
    entries = jax.random.normal(key, shape, jnp.float32) * scale * gain
    return jnp.minimum(jnp.maximum(entries, -most), most).astype(kind)


def setup_inputs(seed: int = 0) -> dict:
    key_of = jax.random.split(jax.random.key(seed), 6)
    queries = draw_queries(jax.random.fold_in(key_of[5], 71), 0)
    keys_in = draw_keys_in(jax.random.fold_in(key_of[5], 71), 0)
    values = gaussian(key_of[2], (TOKENS, D), 1.0, 6.0, ((0, 256),))
    out_grad = gaussian(key_of[3], (TOKENS, D), 1.0, 6.0, ((0, 256),))
    doc_lengths = ragged(key_of[4], DOCS, TOKENS, MAXDOC, 2).astype(jnp.int32)
    return dict(queries=queries, keys_in=keys_in, values=values, out_grad=out_grad, doc_lengths=doc_lengths)


def doc_ids(doc_lengths, positions):
    starts = jnp.cumsum(doc_lengths) - doc_lengths
    return lax.optimization_barrier(jnp.sum((starts[None, :] <= positions[:, None]).astype(jnp.int32), axis=1)) - 1

def block_grads(query_blk, key_win, value_win, grad_blk, allowed, factor):
    scores = jnp.dot(query_blk, key_win.T, preferred_element_type=jnp.float32) * factor
    scores = jnp.where(allowed, scores, -1e+30)
    row_max = lax.optimization_barrier(jnp.max(scores, axis=1, keepdims=True))
    powers = jnp.exp(scores - row_max)
    shares = powers / lax.optimization_barrier(jnp.sum(powers, axis=1, keepdims=True))
    weights = shares.astype(jnp.bfloat16)
    attended = jnp.dot(weights, value_win, preferred_element_type=jnp.float32).astype(jnp.bfloat16)
    attended = lax.optimization_barrier(attended)
    row_delta = lax.optimization_barrier(jnp.sum(grad_blk.astype(jnp.float32) * attended.astype(jnp.float32), axis=1, keepdims=True))
    grad_value = jnp.dot(weights.T, grad_blk, preferred_element_type=jnp.float32)
    grad_prob = jnp.dot(grad_blk, value_win.T, preferred_element_type=jnp.float32)
    grad_score = (shares * (grad_prob - row_delta)).astype(jnp.bfloat16)
    grad_query = jnp.dot(grad_score, key_win, preferred_element_type=jnp.float32) * factor
    grad_key = jnp.dot(grad_score.T, query_blk, preferred_element_type=jnp.float32) * factor
    return (grad_query, grad_key, grad_value)

def sweep(query_head, grad_head, key_ext, value_ext, owners, factor, reach):
    total = query_head.shape[0]
    width = reach + QBLK

    def step(carry, block_index):
        key_acc, value_acc = carry
        start = (block_index * QBLK).astype(jnp.int32)
        query_blk = lax.dynamic_slice_in_dim(query_head, start, QBLK, 0)
        grad_blk = lax.dynamic_slice_in_dim(grad_head, start, QBLK, 0)
        key_win = lax.dynamic_slice_in_dim(key_ext, start, width, 0)
        value_win = lax.dynamic_slice_in_dim(value_ext, start, width, 0)
        owner_query = lax.dynamic_slice_in_dim(owners, start + reach, QBLK, 0)
        owner_key = lax.dynamic_slice_in_dim(owners, start, width, 0)
        causal = jnp.arange(width, dtype=jnp.int32)[None, :] <= jnp.arange(QBLK, dtype=jnp.int32)[:, None] + reach
        allowed = (owner_query[:, None] == owner_key[None, :]) & causal
        grad_query, grad_key, grad_value = block_grads(query_blk, key_win, value_win, grad_blk, allowed, factor)
        key_acc = lax.dynamic_update_slice_in_dim(key_acc, lax.dynamic_slice_in_dim(key_acc, start, width, 0) + grad_key, start, 0)
        value_acc = lax.dynamic_update_slice_in_dim(value_acc, lax.dynamic_slice_in_dim(value_acc, start, width, 0) + grad_value, start, 0)
        return ((key_acc, value_acc), grad_query.astype(jnp.bfloat16))
    zeros = jnp.zeros(key_ext.shape, jnp.float32)
    blocks = jnp.arange(total // QBLK, dtype=jnp.int32)
    (key_acc, value_acc), query_parts = lax.scan(step, (zeros, zeros), blocks)
    return (query_parts.reshape(total, query_head.shape[1]), key_acc, value_acc)

def reference(queries, keys_in, values, out_grad, doc_lengths):
    factor = 1.0 / math.sqrt(HD)
    positions = jnp.arange(-MAXDOC, TOKENS, dtype=jnp.int32)
    owners = doc_ids(doc_lengths, positions)

    def split_heads(array):
        return array.reshape(TOKENS, H, HD).transpose(1, 0, 2)

    def join_heads(array):
        return array.transpose(1, 0, 2).reshape(TOKENS, H * HD)

    def head_grads(stacked):
        query_head, key_head, value_head, grad_head = stacked
        padding = jnp.zeros((MAXDOC, HD), jnp.bfloat16)
        key_ext = jnp.concatenate([padding, key_head], axis=0)
        value_ext = jnp.concatenate([padding, value_head], axis=0)
        grad_query, key_acc, value_acc = sweep(query_head, grad_head, key_ext, value_ext, owners, factor, MAXDOC)
        return (grad_query, key_acc[MAXDOC:].astype(jnp.bfloat16), value_acc[MAXDOC:].astype(jnp.bfloat16))
    grad_query, grad_key, grad_value = lax.map(head_grads, (split_heads(queries), split_heads(keys_in), split_heads(values), split_heads(out_grad)))
    return (join_heads(grad_query), join_heads(grad_key), join_heads(grad_value))
```

```python
import functools, math
import jax
import jax.numpy as jnp
from jax import lax
from jax.experimental import pallas as pl
from jax.experimental.pallas import tpu as pltpu
from jax.sharding import PartitionSpec as P

HD = 96
CH = 128
CQ = 4
CK = 4
FACTOR = 1.0 / math.sqrt(HD)
LOG2 = FACTOR * math.log2(math.e)


def attend_kernel(spec, lens, base, halo, own, qd, dq, back, mine, kvt, kn, vn, score, acc, oacc, qacc):
    nc, docs, cq, ck, q_row, native = spec
    tq, tk = cq * CH, ck * CH
    span = nc * CH
    first = base[0]
    origin = first - span

    def doc_start(position):
        begin, found = jnp.int32(0), jnp.int32(0)
        for d in range(docs):
            found = jnp.where(begin <= position, begin, found)
            begin = begin + lens[d]
        return found - origin

    low_chunk = doc_start(first) // CH
    low_chunk = (low_chunk // ck) * ck

    def stage_halo(c, _):
        block = halo[c]
        kvt[c] = block
        rows = pl.ds(pl.multiple_of(c * CH, CH), CH)
        kn[rows, :] = block[:HD].T
        vn[rows, :] = block[HD:].T
        acc[c] = jnp.zeros((2 * HD, CH), jnp.float32)
        return 0

    def stage_own(c, _):
        block = own[c, : 2 * HD, :]
        kvt[nc + c] = block
        rows = pl.ds(pl.multiple_of((nc + c) * CH, CH), CH)
        kn[rows, :] = block[:HD].T
        vn[rows, :] = block[HD:].T
        acc[nc + c] = jnp.zeros((2 * HD, CH), jnp.float32)
        return 0

    def clear(c, _):
        acc[c] = jnp.zeros((2 * HD, CH), jnp.float32)
        return 0

    lax.fori_loop(0, jnp.minimum(low_chunk, nc), clear, 0)
    lax.fori_loop(low_chunk, nc, stage_halo, 0)
    lax.fori_loop(0, nc, stage_own, 0)

    def wide(ref, chunk, rows, count):
        return jnp.concatenate([ref[chunk + n, rows, :] for n in range(count)], axis=1)

    def q_step(i, _):
        q_chunk = i * cq
        q_begin = span + i * tq
        begin, lo, hi = jnp.int32(0), jnp.int32(0), jnp.int32(0)
        q_pos = q_begin + lax.broadcasted_iota(jnp.int32, (1, tq), 1)
        start_row = jnp.zeros((1, tq), jnp.int32)
        for d in range(docs):
            here = begin - origin
            lo = jnp.where(here <= q_begin, here, lo)
            hi = jnp.where(here <= q_begin + (tq - 1), here, hi)
            start_row = jnp.where(q_pos >= here, here, start_row)
            begin = begin + lens[d]
        k_first = lo // tk
        k_last = (q_begin + tq - 1) // tk + 1
        qt = wide(qd, q_chunk, pl.ds(q_row, HD), cq)
        gt = wide(qd, q_chunk, pl.ds(q_row + HD, HD), cq)

        def score_step(j, top):
            slot = pl.ds(pl.multiple_of((j - k_first) * tk, tk), tk)
            rows = pl.ds(pl.multiple_of(j * tk, tk), tk)
            k_begin = j * tk
            s = jnp.dot(kn[rows, :], qt, preferred_element_type=jnp.float32)
            plain = (k_begin >= hi) & (k_begin + tk <= q_begin)

            def masked(s):
                k_pos = k_begin + lax.broadcasted_iota(jnp.int32, (tk, tq), 0)
                keep = (k_pos >= start_row) & (k_pos <= q_pos)
                return jnp.where(keep, s, -1e30)

            s = lax.cond(plain, lambda s: s, masked, s) if native else masked(s)
            score[slot, :] = s
            return jnp.maximum(top, jnp.max(s.reshape(tk // 8, 8, tq), axis=0))

        top = lax.fori_loop(k_first, k_last, score_step, jnp.full((8, tq), -1e30, jnp.float32))
        top = jnp.max(top, axis=0, keepdims=True)
        oacc[...] = jnp.zeros_like(oacc)

        def power_step(j, total):
            slot = pl.ds(pl.multiple_of((j - k_first) * tk, tk), tk)
            p = jnp.exp2((score[slot, :] - top) * LOG2)
            score[slot, :] = p
            vt = wide(kvt, j * ck, pl.ds(HD, HD), ck)
            oacc[...] += jnp.dot(vt, p.astype(jnp.bfloat16), preferred_element_type=jnp.float32)
            return total + jnp.sum(p.reshape(tk // 8, 8, tq), axis=0)

        total = lax.fori_loop(k_first, k_last, power_step, jnp.zeros((8, tq), jnp.float32))
        inverse = 1.0 / jnp.sum(total, axis=0, keepdims=True)
        attended = (oacc[...] * inverse).astype(jnp.bfloat16).astype(jnp.float32)
        delta = jnp.sum(gt.astype(jnp.float32) * attended, axis=0, keepdims=True)
        qacc[...] = jnp.zeros_like(qacc)

        def grad_step(j, _):
            slot = pl.ds(pl.multiple_of((j - k_first) * tk, tk), tk)
            rows = pl.ds(pl.multiple_of(j * tk, tk), tk)
            shares = score[slot, :] * inverse
            weights = shares.astype(jnp.bfloat16)
            prob = jnp.dot(vn[rows, :], gt, preferred_element_type=jnp.float32)
            grad = (shares * (prob - delta)).astype(jnp.bfloat16)
            kt = wide(kvt, j * ck, pl.ds(0, HD), ck)
            qacc[...] += jnp.dot(kt, grad, preferred_element_type=jnp.float32)
            last = (((1,), (1,)), ((), ()))
            dk = lax.dot_general(qt, grad, last, preferred_element_type=jnp.float32)
            dv = lax.dot_general(gt, weights, last, preferred_element_type=jnp.float32)
            for n in range(ck):
                cols = slice(n * CH, (n + 1) * CH)
                acc[j * ck + n, :HD, :] += dk[:, cols]
                acc[j * ck + n, HD:, :] += dv[:, cols]
            return 0

        lax.fori_loop(k_first, k_last, grad_step, 0)
        out = (qacc[...] * FACTOR).astype(jnp.bfloat16)
        for n in range(cq):
            dq[q_chunk + n] = out[:, n * CH : (n + 1) * CH]
        return 0

    lax.fori_loop(0, nc // cq, q_step, 0)

    def finish(c, _):
        back[c, :HD, :] = (acc[c, :HD, :] * FACTOR).astype(jnp.bfloat16)
        back[c, HD:, :] = acc[c, HD:, :].astype(jnp.bfloat16)
        mine[c, :HD, :] = acc[nc + c, :HD, :] * FACTOR
        mine[c, HD:, :] = acc[nc + c, HD:, :]
        return 0

    lax.fori_loop(0, nc, finish, 0)


def attend(lens, base, halo, own, qd, q_row, cq=2, ck=2, native=True):
    nc = halo.shape[0]
    tq, tk = cq * CH, ck * CH
    window = nc * CH + tq + tk
    spec = (nc, lens.shape[0], cq, ck, q_row, native)
    smem = pl.BlockSpec(memory_space=pltpu.SMEM)
    vmem = pl.BlockSpec(memory_space=pltpu.VMEM)
    return pl.pallas_call(
        functools.partial(attend_kernel, spec),
        out_shape=(
            jax.ShapeDtypeStruct((nc, HD, CH), jnp.bfloat16),
            jax.ShapeDtypeStruct((nc, 2 * HD, CH), jnp.bfloat16),
            jax.ShapeDtypeStruct((nc, 2 * HD, CH), jnp.float32),
        ),
        in_specs=[smem, smem, vmem, vmem, vmem],
        out_specs=(vmem, vmem, vmem),
        scratch_shapes=[
            pltpu.VMEM((2 * nc, 2 * HD, CH), jnp.bfloat16),
            pltpu.VMEM((2 * nc * CH, HD), jnp.bfloat16),
            pltpu.VMEM((2 * nc * CH, HD), jnp.bfloat16),
            pltpu.VMEM((window, tq), jnp.float32),
            pltpu.VMEM((2 * nc, 2 * HD, CH), jnp.float32),
            pltpu.VMEM((HD, tq), jnp.float32),
            pltpu.VMEM((HD, tq), jnp.float32),
        ],
        compiler_params=pltpu.CompilerParams(vmem_limit_bytes=40 * 1024 * 1024),
        name="attend",
    )(lens, base, halo, own, qd)


def pack_kernel(plan, *refs):
    ins, outs = refs[:4], refs[4:]
    for source, (which, row) in zip(ins, plan):
        for m in range(source.shape[1] // (4 * HD)):
            block = source[:, m * 4 * HD : (m + 1) * 4 * HD].T
            for n in range(4):
                outs[which][4 * m + n, row : row + HD, :] = block[n * HD : (n + 1) * HD]


def pack(arrays, half, plan, rows):
    tokens, columns = arrays[0].shape
    half_columns = columns // 2
    peers = half_columns // HD
    return pl.pallas_call(
        functools.partial(pack_kernel, plan),
        grid=(1,),
        out_shape=tuple(jax.ShapeDtypeStruct((peers, r, tokens), jnp.bfloat16) for r in rows),
        in_specs=[pl.BlockSpec((tokens, half_columns), lambda i: (0, half))] * 4,
        out_specs=tuple(pl.BlockSpec((peers, r, tokens), lambda i: (0, 0, 0)) for r in rows),
        compiler_params=pltpu.CompilerParams(vmem_limit_bytes=32 * 1024 * 1024),
        name="pack",
    )(*arrays)


def unpack_kernel(plan, n_in, n_pass, *refs):
    ins, outs = refs[:n_in], refs[n_in + n_pass :]
    for target, (which, row) in zip(outs, plan):
        for m in range(target.shape[1] // (4 * HD)):
            parts = [ins[which][4 * m + n, row : row + HD, :] for n in range(4)]
            target[:, m * 4 * HD : (m + 1) * 4 * HD] = jnp.concatenate(parts, axis=0).T


def unpack(received, half, plan, earlier=()):
    peers, _, tokens = received[0].shape
    columns = 2 * peers * HD
    shape = jax.ShapeDtypeStruct((tokens, columns), jnp.bfloat16)
    n_in, n_pass = len(received), len(earlier)
    return pl.pallas_call(
        functools.partial(unpack_kernel, plan, n_in, n_pass),
        grid=(1,),
        out_shape=(shape,) * len(plan),
        in_specs=[pl.BlockSpec(r.shape, lambda i: (0, 0, 0)) for r in received]
        + [pl.BlockSpec(memory_space=pl.ANY)] * n_pass,
        out_specs=(pl.BlockSpec((tokens, columns // 2), lambda i: (0, half)),) * len(plan),
        input_output_aliases={n_in + n: n for n in range(n_pass)},
        compiler_params=pltpu.CompilerParams(vmem_limit_bytes=32 * 1024 * 1024),
        name="unpack",
    )(*received, *earlier)


def total_kernel(extra, *refs):
    mine, got, out = refs[extra], refs[extra + 1], refs[-1]
    if extra:
        out[:, :HD, :] = refs[0][...]
    base = HD if extra else 0
    out[:, base:, :] = (mine[...] + got[...].astype(jnp.float32)).astype(jnp.bfloat16)


def total(first, mine, got):
    peers, rows, tokens = mine.shape
    extra = len(first)
    return pl.pallas_call(
        functools.partial(total_kernel, extra),
        out_shape=jax.ShapeDtypeStruct((peers, rows + HD * extra, tokens), jnp.bfloat16),
        in_specs=[pl.BlockSpec(memory_space=pltpu.VMEM)] * (2 + extra),
        out_specs=pl.BlockSpec(memory_space=pltpu.VMEM),
        compiler_params=pltpu.CompilerParams(vmem_limit_bytes=32 * 1024 * 1024),
        name="total",
    )(*first, mine, got)


def shards(queries, keys_in, values, out_grad, doc_lengths):
    blocks, group = lax.axis_size("blk"), lax.axis_size("head") // 2
    tokens = queries.shape[0]
    devices = 2 * blocks * group
    halves = [list(range(group)), list(range(group, 2 * group))]
    up = [(i, i + group) for i in range(devices - group)]
    down = [(i + group, i) for i in range(devices - group)]

    def exchange(x):
        return lax.all_to_all(
            x, "head", split_axis=0, concat_axis=0, tiled=True, axis_index_groups=halves
        )

    def shift(x, route):
        return lax.ppermute(x, ("blk", "head"), route)

    def after(x, *earlier):
        return lax.optimization_barrier((x, *earlier))[0]

    half_index = lax.axis_index("blk") * 2 + lax.axis_index("head") // group
    base = (half_index * (group * tokens)).astype(jnp.int32).reshape(1)
    arrays = (keys_in, values, queries, out_grad)
    (send_a,) = pack(arrays, 0, ((0, 0), (0, HD), (0, 2 * HD), (0, 3 * HD)), (4 * HD,))
    send_kv, send_qd = pack(arrays, 1, ((0, 0), (0, HD), (1, 0), (1, HD)), (2 * HD, 2 * HD))

    own_a = exchange(send_a)
    halo_a = shift(own_a[:, : 2 * HD, :], up)
    own_b = exchange(after(send_kv, own_a))
    halo_b = shift(own_b, up)
    rows_b = exchange(after(send_qd, own_b, halo_a))

    dq_a, back_a, mine_a = attend(doc_lengths, base, after(halo_a, own_b), own_a, own_a, 2 * HD, CQ, CK, False)
    got_a = shift(back_a, down)
    out_qa = exchange(after(dq_a, rows_b, halo_b))
    dq_b, back_b, mine_b = attend(doc_lengths, base, halo_b, own_b, rows_b, 0, CQ, CK, False)
    got_b = shift(back_b, down)
    out_ab = exchange(after(total((dq_b,), mine_a, got_a), out_qa))
    out_b = exchange(after(total((), mine_b, got_b), out_ab))
    early = unpack((out_qa, out_ab), 0, ((0, 0), (1, HD), (1, 2 * HD)))
    return unpack((out_ab, out_b), 1, ((0, 0), (1, 0), (1, HD)), early)


def solution(mesh):
    rows = P(("blk", "head"), None)
    return jax.shard_map(
        shards,
        mesh=mesh,
        in_specs=(rows, rows, rows, rows, P()),
        out_specs=(rows, rows, rows),
        check_vma=False,
    )
```

```python
import functools, math
import jax
import jax.numpy as jnp
from jax import lax
from jax.experimental import pallas as pl
from jax.experimental.pallas import tpu as pltpu
from jax.sharding import PartitionSpec as P

HD = 96
CH = 128
CQ = 4
CK = 2
PACK_VMEM = 56 * 1024 * 1024
TOTAL_VMEM = 16 * 1024 * 1024
SUB = 2
RUNS = (4, 2, 1)
ATTEND_VMEM = 40 * 1024 * 1024
FACTOR = 1.0 / math.sqrt(HD)
LOG2 = FACTOR * math.log2(math.e)


def attend_kernel(spec, lens, base, halo, own, qd, *refs):
    dq, back, mine = refs[-10:-7]
    (kvt, kn, vn, score, acc, oacc, qacc) = refs[-7:]
    nc, docs, cq, ck, q_row, native = spec
    tq, tk = cq * CH, ck * CH
    span = nc * CH
    first = base[0]
    origin = first - span

    def doc_start(position):
        begin, found = jnp.int32(0), jnp.int32(0)
        for d in range(docs):
            found = jnp.where(begin <= position, begin, found)
            begin = begin + lens[d]
        return found - origin

    low_chunk = doc_start(first) // CH
    low_chunk = (low_chunk // ck) * ck

    def stage_halo(c, _):
        block = halo[c]
        kvt[c] = block
        rows = pl.ds(pl.multiple_of(c * CH, CH), CH)
        kn[rows, :] = block[:HD].T
        vn[rows, :] = block[HD:].T
        acc[c] = jnp.zeros((2 * HD, CH), jnp.float32)
        return 0

    def stage_own(c, _):
        block = own[c, : 2 * HD, :]
        kvt[nc + c] = block
        rows = pl.ds(pl.multiple_of((nc + c) * CH, CH), CH)
        kn[rows, :] = block[:HD].T
        vn[rows, :] = block[HD:].T
        acc[nc + c] = jnp.zeros((2 * HD, CH), jnp.float32)
        return 0

    def clear(c, _):
        acc[c] = jnp.zeros((2 * HD, CH), jnp.float32)
        return 0

    step = pl.program_id(0)

    @pl.when(step == 0)
    def _():
        lax.fori_loop(0, jnp.minimum(low_chunk, nc), clear, 0)
        lax.fori_loop(low_chunk, nc, stage_halo, 0)
        lax.fori_loop(0, nc, stage_own, 0, unroll=2)


    def wide(ref, chunk, rows, count):
        return jnp.concatenate([ref[chunk + n, rows, :] for n in range(count)], axis=1)

    def q_step(i):
        q_chunk = i * cq
        q_begin = span + i * tq
        begin, lo, hi = jnp.int32(0), jnp.int32(0), jnp.int32(0)
        q_pos = q_begin + lax.broadcasted_iota(jnp.int32, (1, tq), 1)
        start_row = jnp.zeros((1, tq), jnp.int32)
        for d in range(docs):
            here = begin - origin
            lo = jnp.where(here <= q_begin, here, lo)
            hi = jnp.where(here <= q_begin + (tq - 1), here, hi)
            start_row = jnp.where(q_pos >= here, here, start_row)
            begin = begin + lens[d]
        k_first = lo // tk
        k_last = (q_begin + tq - 1) // tk + 1
        qt = wide(qd, q_chunk, pl.ds(q_row, HD), cq)
        gt = wide(qd, q_chunk, pl.ds(q_row + HD, HD), cq)

        def rows_of(j, n):
            return pl.ds(pl.multiple_of(j * tk + n * CH * SUB, CH * SUB), CH * SUB)

        def slot_of(j, n):
            return pl.ds(pl.multiple_of((j - k_first) * tk + n * CH * SUB, CH * SUB), CH * SUB)

        size = CH * SUB

        def sweep(step, carry):
            j = k_first
            for run in RUNS:
                count = (k_last - j) // run
                parts = run * ck // SUB
                carry = lax.fori_loop(0, count, lambda t, c: step(j + t * run, parts, c), carry)
                j = j + count * run
            return carry

        def score_step(j, parts, top):
            def product(n):
                return jnp.dot(kn[rows_of(j, n), :], qt, preferred_element_type=jnp.float32)

            s = product(0)
            for n in range(parts):
                later = product(n + 1) if n + 1 < parts else None
                k_pos = j * tk + n * size + lax.broadcasted_iota(jnp.int32, (size, tq), 0)
                s = jnp.where((k_pos >= start_row) & (k_pos <= q_pos), s, -1e30)
                score[slot_of(j, n), :] = s
                top = jnp.maximum(top, jnp.max(s.reshape(size // 8, 8, tq), axis=0))
                s = later
            return top

        top = sweep(score_step, jnp.full((8, tq), -1e30, jnp.float32))
        top = jnp.max(top, axis=0, keepdims=True)
        oacc[...] = jnp.zeros_like(oacc)

        def power_step(j, parts, total):
            out, held = None, None
            for n in range(parts + 1):
                if n < parts:
                    p = jnp.exp2((score[slot_of(j, n), :] - top) * LOG2)
                    score[slot_of(j, n), :] = p
                    total = total + jnp.sum(p.reshape(size // 8, 8, tq), axis=0)
                    narrow = p.astype(jnp.bfloat16)
                if n:
                    vt = wide(kvt, j * ck + (n - 1) * SUB, pl.ds(HD, HD), SUB)
                    term = jnp.dot(vt, held, preferred_element_type=jnp.float32)
                    out = term if out is None else out + term
                held = narrow
            oacc[...] += out
            return total

        total = sweep(power_step, jnp.zeros((8, tq), jnp.float32))
        inverse = 1.0 / jnp.sum(total, axis=0, keepdims=True)
        attended = (oacc[...] * inverse).astype(jnp.bfloat16).astype(jnp.float32)
        delta = jnp.sum(gt.astype(jnp.float32) * attended, axis=0, keepdims=True)
        qacc[...] = jnp.zeros_like(qacc)

        def grad_step(j, parts, _):
            last = (((1,), (1,)), ((), ()))

            def product(n):
                return jnp.dot(vn[rows_of(j, n), :], gt, preferred_element_type=jnp.float32)

            prob, held, out = product(0), None, None
            for n in range(parts + 1):
                later = product(n + 1) if n + 1 < parts else None
                if n < parts:
                    shares = score[slot_of(j, n), :] * inverse
                    weights = shares.astype(jnp.bfloat16)
                    grad = (shares * (prob - delta)).astype(jnp.bfloat16)
                if n:
                    old_weights, old_grad = held
                    m = j * ck + (n - 1) * SUB
                    kt = wide(kvt, m, pl.ds(0, HD), SUB)
                    term = jnp.dot(kt, old_grad, preferred_element_type=jnp.float32)
                    out = term if out is None else out + term
                    dk = lax.dot_general(qt, old_grad, last, preferred_element_type=jnp.float32)
                    dv = lax.dot_general(gt, old_weights, last, preferred_element_type=jnp.float32)
                    for c in range(SUB):
                        cols = slice(c * CH, (c + 1) * CH)
                        acc[m + c, :HD, :] += dk[:, cols]
                        acc[m + c, HD:, :] += dv[:, cols]
                held = (weights, grad)
                prob = later
            qacc[...] += out
            return 0

        sweep(grad_step, 0)
        out = (qacc[...] * FACTOR).astype(jnp.bfloat16)
        for n in range(cq):
            dq[n] = out[:, n * CH : (n + 1) * CH]
            done = acc[i * cq + n]
            back[n, :HD, :] = (done[:HD] * FACTOR).astype(jnp.bfloat16)
            back[n, HD:, :] = done[HD:].astype(jnp.bfloat16)

    q_step(step)

    @pl.when(step == nc // cq - 1)
    def _():
        def finish(c, _):
            mine[c, :HD, :] = acc[nc + c, :HD, :] * FACTOR
            mine[c, HD:, :] = acc[nc + c, HD:, :]
            return 0

        lax.fori_loop(0, nc, finish, 0, unroll=2)


def attend(lens, base, halo, own, qd, q_row, cq=2, ck=2, native=True, carried=()):
    nc = halo.shape[0]
    tq, tk = cq * CH, ck * CH
    window = nc * CH + tq + tk
    spec = (nc, lens.shape[0], cq, ck, q_row, native)
    smem = pl.BlockSpec(memory_space=pltpu.SMEM)

    def whole(x):
        return pl.BlockSpec(x.shape, lambda i: (0, 0, 0))

    def part(rows):
        return pl.BlockSpec((cq, rows, CH), lambda i: (i, 0, 0))

    through = [pl.BlockSpec(memory_space=pl.ANY)] * len(carried)
    return pl.pallas_call(
        functools.partial(attend_kernel, spec),
        grid=(nc // cq,),
        out_shape=tuple(jax.ShapeDtypeStruct(x.shape, x.dtype) for x in carried)
        + (
            jax.ShapeDtypeStruct((nc, HD, CH), jnp.bfloat16),
            jax.ShapeDtypeStruct((nc, 2 * HD, CH), jnp.bfloat16),
            jax.ShapeDtypeStruct((nc, 2 * HD, CH), jnp.float32),
        ),
        in_specs=[smem, smem, whole(halo), whole(own), whole(qd)] + through,
        input_output_aliases={5 + n: n for n in range(len(carried))},
        out_specs=tuple(through)
        + (
            part(HD),
            part(2 * HD),
            pl.BlockSpec((nc, 2 * HD, CH), lambda i: (0, 0, 0)),
        ),
        scratch_shapes=[
            pltpu.VMEM((2 * nc, 2 * HD, CH), jnp.bfloat16),
            pltpu.VMEM((2 * nc * CH, HD), jnp.bfloat16),
            pltpu.VMEM((2 * nc * CH, HD), jnp.bfloat16),
            pltpu.VMEM((window, tq), jnp.float32),
            pltpu.VMEM((2 * nc, 2 * HD, CH), jnp.float32),
            pltpu.VMEM((HD, tq), jnp.float32),
            pltpu.VMEM((HD, tq), jnp.float32),
        ],
        compiler_params=pltpu.CompilerParams(vmem_limit_bytes=ATTEND_VMEM),
        name="attend",
    )(lens, base, halo, own, qd, *carried)


def pack_kernel(plan, *refs):
    ins, outs = refs[: len(plan)], refs[len(plan) :]
    for source, (which, row) in zip(ins, plan):
        for m in range(source.shape[1] // (4 * HD)):
            block = source[:, m * 4 * HD : (m + 1) * 4 * HD].T
            for n in range(4):
                outs[which][4 * m + n, row : row + HD, :] = block[n * HD : (n + 1) * HD]


def pack(arrays, half, plan, rows):
    tokens, columns = arrays[0].shape
    peers = columns // (2 * HD)
    steps = peers // 4
    return pl.pallas_call(
        functools.partial(pack_kernel, plan),
        grid=(steps,),
        out_shape=tuple(jax.ShapeDtypeStruct((peers, r, tokens), jnp.bfloat16) for r in rows),
        in_specs=[pl.BlockSpec((tokens, 4 * HD), lambda i: (0, half * steps + i))] * len(arrays),
        out_specs=tuple(pl.BlockSpec((4, r, tokens), lambda i: (i, 0, 0)) for r in rows),
        compiler_params=pltpu.CompilerParams(vmem_limit_bytes=PACK_VMEM),
        name="pack",
    )(*arrays)


def unpack_kernel(plan, n_in, n_pass, *refs):
    ins, outs = refs[:n_in], refs[n_in + n_pass :]
    for target, (which, row) in zip(outs, plan):
        for m in range(target.shape[1] // (4 * HD)):
            parts = [ins[which][4 * m + n, row : row + HD, :] for n in range(4)]
            target[:, m * 4 * HD : (m + 1) * 4 * HD] = jnp.concatenate(parts, axis=0).T


def unpack(received, half, plan, earlier=()):
    peers, _, tokens = received[0].shape
    columns = 2 * peers * HD
    shape = jax.ShapeDtypeStruct((tokens, columns), jnp.bfloat16)
    n_in, n_pass = len(received), len(earlier)
    return pl.pallas_call(
        functools.partial(unpack_kernel, plan, n_in, n_pass),
        grid=(1,),
        out_shape=(shape,) * len(plan),
        in_specs=[pl.BlockSpec(r.shape, lambda i: (0, 0, 0)) for r in received]
        + [pl.BlockSpec(memory_space=pl.ANY)] * n_pass,
        out_specs=(pl.BlockSpec((tokens, columns // 2), lambda i: (0, half)),) * len(plan),
        input_output_aliases={n_in + n: n for n in range(n_pass)},
        compiler_params=pltpu.CompilerParams(vmem_limit_bytes=32 * 1024 * 1024),
        name="unpack",
    )(*received, *earlier)


def total_kernel(extra, *refs):
    mine, got, out = refs[extra], refs[extra + 1], refs[-1]
    if extra:
        out[:, :HD, :] = refs[0][...]
    base = HD if extra else 0
    out[:, base:, :] = (mine[...] + got[...].astype(jnp.float32)).astype(jnp.bfloat16)


def total(first, mine, got):
    peers, rows, tokens = mine.shape
    extra = len(first)
    steps = 2

    def part(height):
        return pl.BlockSpec((peers // steps, height, tokens), lambda i: (i, 0, 0))

    return pl.pallas_call(
        functools.partial(total_kernel, extra),
        grid=(steps,),
        out_shape=jax.ShapeDtypeStruct((peers, rows + HD * extra, tokens), jnp.bfloat16),
        in_specs=[part(HD)] * extra + [part(rows)] * 2,
        out_specs=part(rows + HD * extra),
        compiler_params=pltpu.CompilerParams(vmem_limit_bytes=TOTAL_VMEM),
        name="total",
    )(*first, mine, got)


def shards(queries, keys_in, values, out_grad, doc_lengths):
    blocks, group = lax.axis_size("blk"), lax.axis_size("head") // 2
    tokens = queries.shape[0]
    devices = 2 * blocks * group
    halves = [list(range(group)), list(range(group, 2 * group))]
    up = [(i, i + group) for i in range(devices - group)]
    down = [(i + group, i) for i in range(devices - group)]

    def exchange(x):
        return lax.all_to_all(
            x, "head", split_axis=0, concat_axis=0, tiled=True, axis_index_groups=halves
        )

    def shift(x, route):
        return lax.ppermute(x, ("blk", "head"), route)

    def after(x, *earlier):
        return lax.optimization_barrier((x, *earlier))[0]

    half_index = lax.axis_index("blk") * 2 + lax.axis_index("head") // group
    base = (half_index * (group * tokens)).astype(jnp.int32).reshape(1)
    pair = ((0, 0), (0, HD))

    def pack_pair(first, second, half):
        return pack((first, second), half, pair, (2 * HD,))[0]

    send_kv_a = pack_pair(keys_in, values, 0)
    send_q_a = pack_pair(queries, out_grad, 0)
    send_kv_b = pack_pair(keys_in, values, 1)
    send_q_b = pack_pair(queries, out_grad, 1)

    own_a = exchange(send_kv_a)
    halo_a = shift(own_a, up)
    rows_a = exchange(after(send_q_a, own_a, send_kv_b, send_q_b))
    own_b = exchange(after(send_kv_b, rows_a, halo_a))
    halo_b = shift(own_b, up)
    send_q_b, dq_a, back_a, mine_a = attend(
        doc_lengths, base, halo_a, own_a, rows_a, 0, CQ, CK, False, (send_q_b,)
    )
    got_a = shift(back_a, down)
    rows_b = exchange(after(send_q_b, own_b))
    sum_a = total((dq_a,), mine_a, got_a)
    out_a = exchange(after(sum_a, rows_b, halo_b))
    dq_b, back_b, mine_b = attend(doc_lengths, base, halo_b, own_b, rows_b, 0, CQ, CK, False)
    got_b = shift(back_b, down)
    out_q = exchange(after(dq_b, out_a))
    sum_b = total((), mine_b, got_b)
    out_b = exchange(after(sum_b, out_q))
    grad_q, grad_k, grad_v = unpack((out_a,), 0, ((0, 0), (0, HD), (0, 2 * HD)))
    (grad_q,) = unpack((out_q,), 1, ((0, 0),), (grad_q,))
    grad_k, grad_v = unpack((out_b,), 1, pair, (grad_k, grad_v))
    return grad_q, grad_k, grad_v


def solution(mesh):
    rows = P(("blk", "head"), None)
    return jax.shard_map(
        shards,
        mesh=mesh,
        in_specs=(rows, rows, rows, rows, P()),
        out_specs=(rows, rows, rows),
        check_vma=False,
    )
```

```python
import functools, math
import jax
import jax.numpy as jnp
from jax import lax
from jax.experimental import pallas as pl
from jax.experimental.pallas import tpu as pltpu
from jax.sharding import PartitionSpec as P

HD = 96
CH = 128
PACK_VMEM = 56 * 1024 * 1024
TOTAL_VMEM = 56 * 1024 * 1024
SUB = 2
ATTEND_VMEM = 40 * 1024 * 1024
FACTOR = 1.0 / math.sqrt(HD)
LOG2 = FACTOR * math.log2(math.e)


def attend_kernel(spec, lens, base, halo, own, qd, *refs):
    dq, back, mine = refs[-10:-7]
    (kvt, kn, vn, score, acc, oacc, qacc) = refs[-7:]
    nc, docs, cq, ck, q_row = spec
    tq, tk = cq * CH, ck * CH
    span = nc * CH
    first = base[0]
    origin = first - span

    def doc_start(position):
        begin, found = jnp.int32(0), jnp.int32(0)
        for d in range(docs):
            found = jnp.where(begin <= position, begin, found)
            begin = begin + lens[d]
        return found - origin

    low_chunk = doc_start(first) // CH
    low_chunk = (low_chunk // ck) * ck

    def stage_halo(c, _):
        block = halo[c]
        kvt[c] = block
        rows = pl.ds(pl.multiple_of(c * CH, CH), CH)
        kn[rows, :] = block[:HD].T
        vn[rows, :] = block[HD:].T
        acc[c] = jnp.zeros((2 * HD, CH), jnp.float32)
        return 0

    def stage_own(c, _):
        block = own[c, : 2 * HD, :]
        kvt[nc + c] = block
        rows = pl.ds(pl.multiple_of((nc + c) * CH, CH), CH)
        kn[rows, :] = block[:HD].T
        vn[rows, :] = block[HD:].T
        acc[nc + c] = jnp.zeros((2 * HD, CH), jnp.float32)
        return 0

    def clear(c, _):
        acc[c] = jnp.zeros((2 * HD, CH), jnp.float32)
        return 0

    step = pl.program_id(0)

    @pl.when(step == 0)
    def _():
        lax.fori_loop(0, jnp.minimum(low_chunk, nc), clear, 0)
        lax.fori_loop(low_chunk, nc, stage_halo, 0)
        lax.fori_loop(0, nc, stage_own, 0, unroll=2)


    def wide(ref, chunk, rows, count):
        return jnp.concatenate([ref[chunk + n, rows, :] for n in range(count)], axis=1)

    def q_step(i):
        q_chunk = i * cq
        q_begin = span + i * tq
        begin, lo = jnp.int32(0), jnp.int32(0)
        q_pos = q_begin + lax.broadcasted_iota(jnp.int32, (1, tq), 1)
        start_row = jnp.zeros((1, tq), jnp.int32)
        for d in range(docs):
            here = begin - origin
            lo = jnp.where(here <= q_begin, here, lo)
            start_row = jnp.where(q_pos >= here, here, start_row)
            begin = begin + lens[d]
        k_first = lo // tk
        k_last = (q_begin + tq - 1) // tk + 1
        qt = wide(qd, q_chunk, pl.ds(q_row, HD), cq)
        gt = wide(qd, q_chunk, pl.ds(q_row + HD, HD), cq)

        def run(count):
            def rows_of(j, n):
                return pl.ds(pl.multiple_of(j * tk + n * CH * SUB, CH * SUB), CH * SUB)

            def slot_of(j, n):
                return pl.ds(n * CH * SUB, CH * SUB)

            size = CH * SUB

            def sweep(step, carry):
                return step(k_first, count * ck // SUB, carry)

            def score_step(j, parts, top):
                def product(n):
                    return jnp.dot(kn[rows_of(j, n), :], qt, preferred_element_type=jnp.float32)

                s = product(0)
                for n in range(parts):
                    later = product(n + 1) if n + 1 < parts else None
                    k_pos = j * tk + n * size + lax.broadcasted_iota(jnp.int32, (size, tq), 0)
                    keep = k_pos >= start_row
                    if (n + 1) * size > count * tk - tq:
                        keep = keep & (k_pos <= q_pos)
                    s = jnp.where(keep, s, -1e30)
                    score[slot_of(j, n), :] = s
                    top = jnp.maximum(top, jnp.max(s.reshape(size // 8, 8, tq), axis=0))
                    s = later
                return top

            top = sweep(score_step, jnp.full((8, tq), -1e30, jnp.float32))
            top = jnp.max(top, axis=0, keepdims=True)
            oacc[...] = jnp.zeros_like(oacc)

            def power_step(j, parts, total):
                out, held = None, None
                for n in range(parts + 1):
                    if n < parts:
                        p = jnp.exp2((score[slot_of(j, n), :] - top) * LOG2)
                        score[slot_of(j, n), :] = p
                        total = total + jnp.sum(p.reshape(size // 8, 8, tq), axis=0)
                        narrow = p.astype(jnp.bfloat16)
                    if n:
                        vt = wide(kvt, j * ck + (n - 1) * SUB, pl.ds(HD, HD), SUB)
                        term = jnp.dot(vt, held, preferred_element_type=jnp.float32)
                        out = term if out is None else out + term
                    held = narrow
                oacc[...] += out
                return total

            total = sweep(power_step, jnp.zeros((8, tq), jnp.float32))
            inverse = 1.0 / jnp.sum(total, axis=0, keepdims=True)
            attended = (oacc[...] * inverse).astype(jnp.bfloat16).astype(jnp.float32)
            delta = jnp.sum(gt.astype(jnp.float32) * attended, axis=0, keepdims=True)
            qacc[...] = jnp.zeros_like(qacc)

            def grad_step(j, parts, _):
                last = (((1,), (1,)), ((), ()))

                def product(n):
                    return jnp.dot(vn[rows_of(j, n), :], gt, preferred_element_type=jnp.float32)

                prob, held, out = product(0), None, None
                for n in range(parts + 1):
                    later = product(n + 1) if n + 1 < parts else None
                    if n < parts:
                        shares = score[slot_of(j, n), :] * inverse
                        weights = shares.astype(jnp.bfloat16)
                        grad = (shares * (prob - delta)).astype(jnp.bfloat16)
                    if n:
                        old_weights, old_grad = held
                        m = j * ck + (n - 1) * SUB
                        kt = wide(kvt, m, pl.ds(0, HD), SUB)
                        term = jnp.dot(kt, old_grad, preferred_element_type=jnp.float32)
                        out = term if out is None else out + term
                        dk = lax.dot_general(qt, old_grad, last, preferred_element_type=jnp.float32)
                        dv = lax.dot_general(gt, old_weights, last, preferred_element_type=jnp.float32)
                        for c in range(SUB):
                            cols = slice(c * CH, (c + 1) * CH)
                            acc[m + c, :HD, :] += dk[:, cols]
                            acc[m + c, HD:, :] += dv[:, cols]
                    held = (weights, grad)
                    prob = later
                qacc[...] += out
                return 0

            sweep(grad_step, 0)
            out = (qacc[...] * FACTOR).astype(jnp.bfloat16)
            for n in range(cq):
                dq[n] = out[:, n * CH : (n + 1) * CH]
                done = acc[nc + i * cq + n]
                mine[n, :HD, :] = done[:HD] * FACTOR
                mine[n, HD:, :] = done[HD:]

        for count in range(1, (nc * CH + tq - 1) // tk + 2):
            pl.when(k_last - k_first == count)(functools.partial(run, count))

    q_step(nc // cq - 1 - step)

    @pl.when(step == nc // cq - 1)
    def _():
        def finish(c, _):
            back[c, :HD, :] = (acc[c, :HD, :] * FACTOR).astype(jnp.bfloat16)
            back[c, HD:, :] = acc[c, HD:, :].astype(jnp.bfloat16)
            return 0

        lax.fori_loop(0, nc, finish, 0, unroll=2)


def attend(lens, base, halo, own, qd, q_row, into=None, cq=2, ck=2):
    nc = halo.shape[0]
    tq, tk = cq * CH, ck * CH
    window = nc * CH + tq + tk
    spec = (nc, lens.shape[0], cq, ck, q_row)
    smem = pl.BlockSpec(memory_space=pltpu.SMEM)

    steps = nc // cq

    def whole(x):
        return pl.BlockSpec(x.shape, lambda i: (0, 0, 0))

    def part(rows):
        return pl.BlockSpec((cq, rows, CH), lambda i: (steps - 1 - i, 0, 0))

    through, extra, target, slot = [], (), (nc, HD, CH), 0
    if into is not None:
        through, extra, target = [pl.BlockSpec(memory_space=pl.ANY)], (into,), into.shape
        slot = into.shape[1] // HD - 1
    return pl.pallas_call(
        functools.partial(attend_kernel, spec),
        grid=(nc // cq,),
        out_shape=(
            pltpu.HBM(target, jnp.bfloat16),
            jax.ShapeDtypeStruct((nc, 2 * HD, CH), jnp.bfloat16),
            pltpu.HBM((nc, 2 * HD, CH), jnp.float32),
        ),
        in_specs=[smem, smem, whole(halo), whole(own), whole(qd)] + through,
        input_output_aliases={5: 0} if extra else {},
        out_specs=(
            pl.BlockSpec((cq, HD, CH), lambda i: (steps - 1 - i, slot, 0)),
            pl.BlockSpec((nc, 2 * HD, CH), lambda i: (0, 0, 0)),
            part(2 * HD),
        ),
        scratch_shapes=[
            pltpu.VMEM((2 * nc, 2 * HD, CH), jnp.bfloat16),
            pltpu.VMEM((2 * nc * CH, HD), jnp.bfloat16),
            pltpu.VMEM((2 * nc * CH, HD), jnp.bfloat16),
            pltpu.VMEM((window, tq), jnp.float32),
            pltpu.VMEM((2 * nc, 2 * HD, CH), jnp.float32),
            pltpu.VMEM((HD, tq), jnp.float32),
            pltpu.VMEM((HD, tq), jnp.float32),
        ],
        compiler_params=pltpu.CompilerParams(vmem_limit_bytes=ATTEND_VMEM),
        name="attend",
    )(lens, base, halo, own, qd, *extra)


def pack_kernel(plan, *refs):
    ins, outs = refs[: len(plan)], refs[len(plan) :]
    for source, (which, row) in zip(ins, plan):
        for m in range(source.shape[1] // (4 * HD)):
            block = source[:, m * 4 * HD : (m + 1) * 4 * HD].T
            for n in range(4):
                outs[which][4 * m + n, row : row + HD, :] = block[n * HD : (n + 1) * HD]


def pack(arrays, half, plan, rows):
    tokens, columns = arrays[0].shape
    peers = columns // (2 * HD)
    steps = peers // 4
    return pl.pallas_call(
        functools.partial(pack_kernel, plan),
        grid=(steps,),
        out_shape=tuple(jax.ShapeDtypeStruct((peers, r, tokens), jnp.bfloat16) for r in rows),
        in_specs=[pl.BlockSpec((tokens, 4 * HD), lambda i: (0, half * steps + i))] * len(arrays),
        out_specs=tuple(pl.BlockSpec((4, r, tokens), lambda i: (i, 0, 0)) for r in rows),
        compiler_params=pltpu.CompilerParams(vmem_limit_bytes=PACK_VMEM),
        name="pack",
    )(*arrays)


def unpack_kernel(plan, n_in, n_pass, *refs):
    ins, outs = refs[:n_in], refs[n_in + n_pass :]
    for target, (which, row) in zip(outs, plan):
        for m in range(target.shape[1] // (4 * HD)):
            parts = [ins[which][4 * m + n, row : row + HD, :] for n in range(4)]
            target[:, m * 4 * HD : (m + 1) * 4 * HD] = jnp.concatenate(parts, axis=0).T


def unpack(received, half, plan, earlier=()):
    peers, _, tokens = received[0].shape
    columns = 2 * peers * HD
    shape = jax.ShapeDtypeStruct((tokens, columns), jnp.bfloat16)
    n_in, n_pass = len(received), len(earlier)
    return pl.pallas_call(
        functools.partial(unpack_kernel, plan, n_in, n_pass),
        grid=(1,),
        out_shape=(shape,) * len(plan),
        in_specs=[pl.BlockSpec(r.shape, lambda i: (0, 0, 0)) for r in received]
        + [pl.BlockSpec(memory_space=pl.ANY)] * n_pass,
        out_specs=(pl.BlockSpec((tokens, columns // 2), lambda i: (0, half)),) * len(plan),
        input_output_aliases={n_in + n: n for n in range(n_pass)},
        compiler_params=pltpu.CompilerParams(vmem_limit_bytes=32 * 1024 * 1024),
        name="unpack",
    )(*received, *earlier)


def total_kernel(extra, *refs):
    mine, got, out = refs[extra], refs[extra + 1], refs[-1]
    if extra:
        out[:, :HD, :] = refs[0][...]
    base = HD if extra else 0
    out[:, base:, :] = (mine[...] + got[...].astype(jnp.float32)).astype(jnp.bfloat16)


def total(first, mine, got):
    peers, rows, tokens = mine.shape
    extra = len(first)
    steps = 2

    def part(height):
        return pl.BlockSpec((peers // steps, height, tokens), lambda i: (i, 0, 0))

    return pl.pallas_call(
        functools.partial(total_kernel, extra),
        grid=(steps,),
        out_shape=jax.ShapeDtypeStruct((peers, rows + HD * extra, tokens), jnp.bfloat16),
        in_specs=[part(HD)] * extra + [part(rows)] * 2,
        out_specs=part(rows + HD * extra),
        compiler_params=pltpu.CompilerParams(vmem_limit_bytes=TOTAL_VMEM),
        name="total",
    )(*first, mine, got)


def shards(queries, keys_in, values, out_grad, doc_lengths):
    blocks, group = lax.axis_size("blk"), lax.axis_size("head") // 2
    tokens = queries.shape[0]
    devices = 2 * blocks * group
    halves = [list(range(group)), list(range(group, 2 * group))]
    up = [(i, i + group) for i in range(devices - group)]
    down = [(i + group, i) for i in range(devices - group)]

    def exchange(x):
        return lax.all_to_all(
            x, "head", split_axis=0, concat_axis=0, tiled=True, axis_index_groups=halves
        )

    def shift(x, route):
        return lax.ppermute(x, ("blk", "head"), route)

    def after(x, *earlier):
        return lax.optimization_barrier((x, *earlier))[0]

    half_index = lax.axis_index("blk") * 2 + lax.axis_index("head") // group
    base = (half_index * (group * tokens)).astype(jnp.int32).reshape(1)
    pair = ((0, 0), (0, HD))

    def pack_pair(first, second, half):
        return pack((first, second), half, pair, (2 * HD,))[0]

    send_kv_a = pack_pair(keys_in, values, 0)
    send_q_a = pack_pair(queries, out_grad, 0)
    send_kv_b = pack_pair(keys_in, values, 1)
    send_q_b = pack_pair(queries, out_grad, 1)

    own_a = exchange(send_kv_a)
    halo_a = shift(own_a, up)
    rows_a = exchange(after(send_q_a, own_a, send_kv_b, send_q_b))
    own_b = exchange(after(send_kv_b, rows_a, halo_a))
    halo_b = shift(own_b, up)
    dq_a, back_a, mine_a = attend(doc_lengths, base, halo_a, own_a, rows_a, 0)
    got_a = shift(back_a, down)
    rows_b = exchange(after(send_q_b, own_b, dq_a))
    sum_a = total((dq_a,), mine_a, got_a)
    out_a = exchange(after(sum_a, rows_b, halo_b))
    dq_b, back_b, mine_b = attend(doc_lengths, base, halo_b, own_b, rows_b, 0)
    got_b = shift(back_b, down)
    out_q = exchange(after(dq_b, out_a))
    sum_b = total((), mine_b, got_b)
    out_b = exchange(after(sum_b, out_q))
    grad_q, grad_k, grad_v = unpack((out_a,), 0, ((0, 0), (0, HD), (0, 2 * HD)))
    (grad_q,) = unpack((out_q,), 1, ((0, 0),), (grad_q,))
    grad_k, grad_v = unpack((out_b,), 1, pair, (grad_k, grad_v))
    return grad_q, grad_k, grad_v


def solution(mesh):
    rows = P(("blk", "head"), None)
    return jax.shard_map(
        shards,
        mesh=mesh,
        in_specs=(rows, rows, rows, rows, P()),
        out_specs=(rows, rows, rows),
        check_vma=False,
    )
```

```python
import functools, math
import jax
import jax.numpy as jnp
from jax import lax
from jax.experimental import pallas as pl
from jax.experimental.pallas import tpu as pltpu
from jax.sharding import PartitionSpec as P

HD = 96
CH = 128
PACK_VMEM = 56 * 1024 * 1024
TOTAL_VMEM = 16 * 1024 * 1024
SUB = 2
ATTEND_VMEM = 40 * 1024 * 1024
FACTOR = 1.0 / math.sqrt(HD)
LOG2 = FACTOR * math.log2(math.e)


def attend_kernel(spec, lens, base, halo, own, qd, *refs):
    dq, back, mine = refs[-10:-7]
    (kvt, kn, vn, score, acc, oacc, qacc) = refs[-7:]
    nc, docs, cq, ck, q_row = spec
    tq, tk = cq * CH, ck * CH
    span = nc * CH
    first = base[0]
    origin = first - span

    def doc_start(position):
        begin, found = jnp.int32(0), jnp.int32(0)
        for d in range(docs):
            found = jnp.where(begin <= position, begin, found)
            begin = begin + lens[d]
        return found - origin

    low_chunk = doc_start(first) // CH
    low_chunk = (low_chunk // ck) * ck

    def stage_halo(c, _):
        block = halo[c]
        kvt[c] = block
        rows = pl.ds(pl.multiple_of(c * CH, CH), CH)
        kn[rows, :] = block[:HD].T
        vn[rows, :] = block[HD:].T
        acc[c] = jnp.zeros((2 * HD, CH), jnp.float32)
        return 0

    def stage_own(c, _):
        block = own[c, : 2 * HD, :]
        kvt[nc + c] = block
        rows = pl.ds(pl.multiple_of((nc + c) * CH, CH), CH)
        kn[rows, :] = block[:HD].T
        vn[rows, :] = block[HD:].T
        acc[nc + c] = jnp.zeros((2 * HD, CH), jnp.float32)
        return 0

    def clear(c, _):
        acc[c] = jnp.zeros((2 * HD, CH), jnp.float32)
        return 0

    step = pl.program_id(0)

    @pl.when(step == 0)
    def _():
        lax.fori_loop(0, jnp.minimum(low_chunk, nc), clear, 0)
        lax.fori_loop(low_chunk, nc, stage_halo, 0)
        lax.fori_loop(0, nc, stage_own, 0, unroll=2)


    def wide(ref, chunk, rows, count):
        return jnp.concatenate([ref[chunk + n, rows, :] for n in range(count)], axis=1)

    def q_step(i):
        q_chunk = i * cq
        q_begin = span + i * tq
        begin, lo = jnp.int32(0), jnp.int32(0)
        q_pos = q_begin + lax.broadcasted_iota(jnp.int32, (1, tq), 1)
        start_row = jnp.zeros((1, tq), jnp.int32)
        for d in range(docs):
            here = begin - origin
            lo = jnp.where(here <= q_begin, here, lo)
            start_row = jnp.where(q_pos >= here, here, start_row)
            begin = begin + lens[d]
        k_first = lo // tk
        k_last = (q_begin + tq - 1) // tk + 1
        qt = wide(qd, q_chunk, pl.ds(q_row, HD), cq)
        gt = wide(qd, q_chunk, pl.ds(q_row + HD, HD), cq)

        def run(count):
            def rows_of(j, n):
                return pl.ds(pl.multiple_of(j * tk + n * CH * SUB, CH * SUB), CH * SUB)

            def slot_of(j, n):
                return pl.ds(n * CH * SUB, CH * SUB)

            size = CH * SUB

            def sweep(step, carry):
                return step(k_first, count * ck // SUB, carry)

            def score_step(j, parts, top):
                def product(n):
                    return jnp.dot(kn[rows_of(j, n), :], qt, preferred_element_type=jnp.float32)

                s = product(0)
                for n in range(parts):
                    later = product(n + 1) if n + 1 < parts else None
                    k_pos = j * tk + n * size + lax.broadcasted_iota(jnp.int32, (size, tq), 0)
                    keep = k_pos >= start_row
                    if (n + 1) * size > count * tk - tq:
                        keep = keep & (k_pos <= q_pos)
                    s = jnp.where(keep, s, -1e30)
                    score[slot_of(j, n), :] = s
                    top = jnp.maximum(top, jnp.max(s.reshape(size // 8, 8, tq), axis=0))
                    s = later
                return top

            top = sweep(score_step, jnp.full((8, tq), -1e30, jnp.float32))
            top = jnp.max(top, axis=0, keepdims=True)
            oacc[...] = jnp.zeros_like(oacc)

            def power_step(j, parts, total):
                out, held = None, None
                for n in range(parts + 1):
                    if n < parts:
                        p = jnp.exp2((score[slot_of(j, n), :] - top) * LOG2)
                        score[slot_of(j, n), :] = p
                        total = total + jnp.sum(p.reshape(size // 8, 8, tq), axis=0)
                        narrow = p.astype(jnp.bfloat16)
                    if n:
                        vt = wide(kvt, j * ck + (n - 1) * SUB, pl.ds(HD, HD), SUB)
                        term = jnp.dot(vt, held, preferred_element_type=jnp.float32)
                        out = term if out is None else out + term
                    held = narrow
                oacc[...] += out
                return total

            total = sweep(power_step, jnp.zeros((8, tq), jnp.float32))
            inverse = 1.0 / jnp.sum(total, axis=0, keepdims=True)
            attended = (oacc[...] * inverse).astype(jnp.bfloat16).astype(jnp.float32)
            delta = jnp.sum(gt.astype(jnp.float32) * attended, axis=0, keepdims=True)
            qacc[...] = jnp.zeros_like(qacc)

            def grad_step(j, parts, _):
                last = (((1,), (1,)), ((), ()))

                def product(n):
                    return jnp.dot(vn[rows_of(j, n), :], gt, preferred_element_type=jnp.float32)

                prob, held, out = product(0), None, None
                for n in range(parts + 1):
                    later = product(n + 1) if n + 1 < parts else None
                    if n < parts:
                        shares = score[slot_of(j, n), :] * inverse
                        weights = shares.astype(jnp.bfloat16)
                        grad = (shares * (prob - delta)).astype(jnp.bfloat16)
                    if n:
                        old_weights, old_grad = held
                        m = j * ck + (n - 1) * SUB
                        kt = wide(kvt, m, pl.ds(0, HD), SUB)
                        term = jnp.dot(kt, old_grad, preferred_element_type=jnp.float32)
                        out = term if out is None else out + term
                        dk = lax.dot_general(qt, old_grad, last, preferred_element_type=jnp.float32)
                        dv = lax.dot_general(gt, old_weights, last, preferred_element_type=jnp.float32)
                        for c in range(SUB):
                            cols = slice(c * CH, (c + 1) * CH)
                            acc[m + c, :HD, :] += dk[:, cols]
                            acc[m + c, HD:, :] += dv[:, cols]
                    held = (weights, grad)
                    prob = later
                qacc[...] += out
                return 0

            sweep(grad_step, 0)
            out = (qacc[...] * FACTOR).astype(jnp.bfloat16)
            for n in range(cq):
                dq[n] = out[:, n * CH : (n + 1) * CH]
                done = acc[nc + i * cq + n]
                mine[n, :HD, :] = done[:HD] * FACTOR
                mine[n, HD:, :] = done[HD:]

        for count in range(1, (nc * CH + tq - 1) // tk + 2):
            pl.when(k_last - k_first == count)(functools.partial(run, count))

    q_step(nc // cq - 1 - step)

    @pl.when(step == nc // cq - 1)
    def _():
        def finish(c, _):
            back[c, :HD, :] = (acc[c, :HD, :] * FACTOR).astype(jnp.bfloat16)
            back[c, HD:, :] = acc[c, HD:, :].astype(jnp.bfloat16)
            return 0

        lax.fori_loop(0, nc, finish, 0, unroll=2)


def attend(lens, base, halo, own, qd, q_row, into=None, cq=2, ck=2):
    nc = halo.shape[0]
    tq, tk = cq * CH, ck * CH
    window = nc * CH + tq + tk
    spec = (nc, lens.shape[0], cq, ck, q_row)
    smem = pl.BlockSpec(memory_space=pltpu.SMEM)

    steps = nc // cq

    def whole(x):
        return pl.BlockSpec(x.shape, lambda i: (0, 0, 0))

    def part(rows):
        return pl.BlockSpec((cq, rows, CH), lambda i: (steps - 1 - i, 0, 0))

    through, extra, target, slot = [], (), (nc, HD, CH), 0
    if into is not None:
        through, extra, target = [pl.BlockSpec(memory_space=pl.ANY)], (into,), into.shape
        slot = into.shape[1] // HD - 1
    return pl.pallas_call(
        functools.partial(attend_kernel, spec),
        grid=(nc // cq,),
        out_shape=(
            pltpu.HBM(target, jnp.bfloat16),
            jax.ShapeDtypeStruct((nc, 2 * HD, CH), jnp.bfloat16),
            pltpu.HBM((nc, 2 * HD, CH), jnp.float32),
        ),
        in_specs=[smem, smem, whole(halo), whole(own), whole(qd)] + through,
        input_output_aliases={5: 0} if extra else {},
        out_specs=(
            pl.BlockSpec((cq, HD, CH), lambda i: (steps - 1 - i, slot, 0)),
            pl.BlockSpec((nc, 2 * HD, CH), lambda i: (0, 0, 0)),
            part(2 * HD),
        ),
        scratch_shapes=[
            pltpu.VMEM((2 * nc, 2 * HD, CH), jnp.bfloat16),
            pltpu.VMEM((2 * nc * CH, HD), jnp.bfloat16),
            pltpu.VMEM((2 * nc * CH, HD), jnp.bfloat16),
            pltpu.VMEM((window, tq), jnp.float32),
            pltpu.VMEM((2 * nc, 2 * HD, CH), jnp.float32),
            pltpu.VMEM((HD, tq), jnp.float32),
            pltpu.VMEM((HD, tq), jnp.float32),
        ],
        compiler_params=pltpu.CompilerParams(vmem_limit_bytes=ATTEND_VMEM),
        name="attend",
    )(lens, base, halo, own, qd, *extra)


def pack_kernel(plan, *refs):
    ins, outs = refs[: len(plan)], refs[len(plan) :]
    for source, (which, row) in zip(ins, plan):
        for m in range(source.shape[1] // (4 * HD)):
            block = source[:, m * 4 * HD : (m + 1) * 4 * HD].T
            for n in range(4):
                outs[which][4 * m + n, row : row + HD, :] = block[n * HD : (n + 1) * HD]


def pack(arrays, half, plan, rows):
    tokens, columns = arrays[0].shape
    peers = columns // (2 * HD)
    return pl.pallas_call(
        functools.partial(pack_kernel, plan),
        grid=(1,),
        out_shape=tuple(jax.ShapeDtypeStruct((peers, r, tokens), jnp.bfloat16) for r in rows),
        in_specs=[pl.BlockSpec((tokens, columns // 2), lambda i: (0, half))] * len(arrays),
        out_specs=tuple(pl.BlockSpec((peers, r, tokens), lambda i: (0, 0, 0)) for r in rows),
        compiler_params=pltpu.CompilerParams(vmem_limit_bytes=PACK_VMEM),
        name="pack",
    )(*arrays)


def unpack_kernel(plan, n_in, n_pass, *refs):
    ins, outs = refs[:n_in], refs[n_in + n_pass :]
    for target, (which, row) in zip(outs, plan):
        for m in range(target.shape[1] // (4 * HD)):
            parts = [ins[which][4 * m + n, row : row + HD, :] for n in range(4)]
            target[:, m * 4 * HD : (m + 1) * 4 * HD] = jnp.concatenate(parts, axis=0).T


def unpack(received, half, plan, earlier=()):
    peers, _, tokens = received[0].shape
    columns = 2 * peers * HD
    shape = jax.ShapeDtypeStruct((tokens, columns), jnp.bfloat16)
    n_in, n_pass = len(received), len(earlier)
    return pl.pallas_call(
        functools.partial(unpack_kernel, plan, n_in, n_pass),
        grid=(1,),
        out_shape=(shape,) * len(plan),
        in_specs=[pl.BlockSpec(r.shape, lambda i: (0, 0, 0)) for r in received]
        + [pl.BlockSpec(memory_space=pl.ANY)] * n_pass,
        out_specs=(pl.BlockSpec((tokens, columns // 2), lambda i: (0, half)),) * len(plan),
        input_output_aliases={n_in + n: n for n in range(n_pass)},
        compiler_params=pltpu.CompilerParams(vmem_limit_bytes=32 * 1024 * 1024),
        name="unpack",
    )(*received, *earlier)


def total_kernel(extra, *refs):
    mine, got, out = refs[extra], refs[extra + 1], refs[-1]
    if extra:
        out[:, :HD, :] = refs[0][...]
    base = HD if extra else 0
    out[:, base:, :] = (mine[...] + got[...].astype(jnp.float32)).astype(jnp.bfloat16)


def total(first, mine, got):
    peers, rows, tokens = mine.shape
    extra = len(first)
    steps = 2

    def part(height):
        return pl.BlockSpec((peers // steps, height, tokens), lambda i: (i, 0, 0))

    return pl.pallas_call(
        functools.partial(total_kernel, extra),
        grid=(steps,),
        out_shape=jax.ShapeDtypeStruct((peers, rows + HD * extra, tokens), jnp.bfloat16),
        in_specs=[part(HD)] * extra + [part(rows)] * 2,
        out_specs=part(rows + HD * extra),
        compiler_params=pltpu.CompilerParams(vmem_limit_bytes=TOTAL_VMEM),
        name="total",
    )(*first, mine, got)


def shards(queries, keys_in, values, out_grad, doc_lengths):
    blocks, group = lax.axis_size("blk"), lax.axis_size("head") // 2
    tokens = queries.shape[0]
    devices = 2 * blocks * group
    halves = [list(range(group)), list(range(group, 2 * group))]
    up = [(i, i + group) for i in range(devices - group)]
    down = [(i + group, i) for i in range(devices - group)]

    def exchange(x):
        return lax.all_to_all(
            x, "head", split_axis=0, concat_axis=0, tiled=True, axis_index_groups=halves
        )

    def shift(x, route):
        return lax.ppermute(x, ("blk", "head"), route)

    def after(x, *earlier):
        return lax.optimization_barrier((x, *earlier))[0]

    half_index = lax.axis_index("blk") * 2 + lax.axis_index("head") // group
    base = (half_index * (group * tokens)).astype(jnp.int32).reshape(1)
    pair = ((0, 0), (0, HD))

    def pack_pair(first, second, half):
        return pack((first, second), half, pair, (2 * HD,))[0]

    send_kv_a = pack_pair(keys_in, values, 0)
    send_q_a = pack_pair(queries, out_grad, 0)
    send_kv_b = pack_pair(keys_in, values, 1)
    send_q_b = pack_pair(queries, out_grad, 1)

    own_a = exchange(send_kv_a)
    halo_a = shift(own_a, up)
    rows_a = exchange(after(send_q_a, own_a, send_kv_b, send_q_b))
    own_b = exchange(after(send_kv_b, rows_a, halo_a))
    halo_b = shift(own_b, up)
    dq_a, back_a, mine_a = attend(doc_lengths, base, halo_a, own_a, rows_a, 0)
    got_a = shift(back_a, down)
    rows_b = exchange(after(send_q_b, own_b, dq_a))
    sum_a = total((dq_a,), mine_a, got_a)
    out_a = exchange(after(sum_a, rows_b, halo_b))
    dq_b, back_b, mine_b = attend(doc_lengths, base, halo_b, own_b, rows_b, 0)
    got_b = shift(back_b, down)
    out_q = exchange(after(dq_b, out_a))
    sum_b = total((), mine_b, got_b)
    out_b = exchange(after(sum_b, out_q))
    grad_q, grad_k, grad_v = unpack((out_a,), 0, ((0, 0), (0, HD), (0, 2 * HD)))
    (grad_q,) = unpack((out_q,), 1, ((0, 0),), (grad_q,))
    grad_k, grad_v = unpack((out_b,), 1, pair, (grad_k, grad_v))
    return grad_q, grad_k, grad_v


def solution(mesh):
    rows = P(("blk", "head"), None)
    return jax.shard_map(
        shards,
        mesh=mesh,
        in_specs=(rows, rows, rows, rows, P()),
        out_specs=(rows, rows, rows),
        check_vma=False,
    )
```

```python
import functools, math
import jax
import jax.numpy as jnp
from jax import lax
from jax.experimental import pallas as pl
from jax.experimental.pallas import tpu as pltpu
from jax.sharding import PartitionSpec as P

HD = 96
CH = 128
PACK_VMEM = 56 * 1024 * 1024
TOTAL_VMEM = 16 * 1024 * 1024
SUB = 2
ATTEND_VMEM = 40 * 1024 * 1024
FACTOR = 1.0 / math.sqrt(HD)
LOG2 = FACTOR * math.log2(math.e)


def attend_kernel(spec, lens, base, halo, own, qd, *refs):
    dq, back, mine = refs[-10:-7]
    (kvt, kn, vn, score, acc, oacc, qacc) = refs[-7:]
    nc, docs, cq, ck, q_row = spec
    tq, tk = cq * CH, ck * CH
    span = nc * CH
    first = base[0]
    origin = first - span

    def doc_start(position):
        begin, found = jnp.int32(0), jnp.int32(0)
        for d in range(docs):
            found = jnp.where(begin <= position, begin, found)
            begin = begin + lens[d]
        return found - origin

    low_chunk = doc_start(first) // CH
    low_chunk = (low_chunk // ck) * ck

    def stage_halo(c, _):
        block = halo[c]
        kvt[c] = block
        rows = pl.ds(pl.multiple_of(c * CH, CH), CH)
        kn[rows, :] = block[:HD].T
        vn[rows, :] = block[HD:].T
        acc[c] = jnp.zeros((2 * HD, CH), jnp.float32)
        return 0

    def stage_own(c, _):
        block = own[c, : 2 * HD, :]
        kvt[nc + c] = block
        rows = pl.ds(pl.multiple_of((nc + c) * CH, CH), CH)
        kn[rows, :] = block[:HD].T
        vn[rows, :] = block[HD:].T
        acc[nc + c] = jnp.zeros((2 * HD, CH), jnp.float32)
        return 0

    def clear(c, _):
        acc[c] = jnp.zeros((2 * HD, CH), jnp.float32)
        return 0

    step = pl.program_id(0)

    @pl.when(step == 0)
    def _():
        lax.fori_loop(0, jnp.minimum(low_chunk, nc), clear, 0)
        lax.fori_loop(low_chunk, nc, stage_halo, 0)
        lax.fori_loop(0, nc, stage_own, 0, unroll=2)


    def wide(ref, chunk, rows, count):
        return jnp.concatenate([ref[chunk + n, rows, :] for n in range(count)], axis=1)

    def q_step(i):
        q_chunk = i * cq
        q_begin = span + i * tq
        begin, lo = jnp.int32(0), jnp.int32(0)
        q_pos = q_begin + lax.broadcasted_iota(jnp.int32, (1, tq), 1)
        start_row = jnp.zeros((1, tq), jnp.int32)
        for d in range(docs):
            here = begin - origin
            lo = jnp.where(here <= q_begin, here, lo)
            start_row = jnp.where(q_pos >= here, here, start_row)
            begin = begin + lens[d]
        k_first = lo // tk
        k_last = (q_begin + tq - 1) // tk + 1
        qt = wide(qd, q_chunk, pl.ds(q_row, HD), cq)
        gt = wide(qd, q_chunk, pl.ds(q_row + HD, HD), cq)

        def run(count):
            def rows_of(j, n):
                return pl.ds(pl.multiple_of(j * tk + n * CH * SUB, CH * SUB), CH * SUB)

            def slot_of(j, n):
                return pl.ds(n * CH * SUB, CH * SUB)

            size = CH * SUB

            def sweep(step, carry):
                return step(k_first, count * ck // SUB, carry)

            def score_step(j, parts, top):
                def product(n):
                    return jnp.dot(kn[rows_of(j, n), :], qt, preferred_element_type=jnp.float32)

                s = product(0)
                for n in range(parts):
                    later = product(n + 1) if n + 1 < parts else None
                    k_pos = j * tk + n * size + lax.broadcasted_iota(jnp.int32, (size, tq), 0)
                    keep = k_pos >= start_row
                    if (n + 1) * size > count * tk - tq:
                        keep = keep & (k_pos <= q_pos)
                    s = jnp.where(keep, s, -1e30)
                    score[slot_of(j, n), :] = s
                    top = jnp.maximum(top, jnp.max(s.reshape(size // 8, 8, tq), axis=0))
                    s = later
                return top

            top = sweep(score_step, jnp.full((8, tq), -1e30, jnp.float32))
            top = jnp.max(top, axis=0, keepdims=True)
            oacc[...] = jnp.zeros_like(oacc)

            def power_step(j, parts, total):
                out, held = None, None
                for n in range(parts + 1):
                    if n < parts:
                        p = jnp.exp2((score[slot_of(j, n), :] - top) * LOG2)
                        score[slot_of(j, n), :] = p
                        total = total + jnp.sum(p.reshape(size // 8, 8, tq), axis=0)
                        narrow = p.astype(jnp.bfloat16)
                    if n:
                        vt = wide(kvt, j * ck + (n - 1) * SUB, pl.ds(HD, HD), SUB)
                        term = jnp.dot(vt, held, preferred_element_type=jnp.float32)
                        out = term if out is None else out + term
                    held = narrow
                oacc[...] += out
                return total

            total = sweep(power_step, jnp.zeros((8, tq), jnp.float32))
            inverse = 1.0 / jnp.sum(total, axis=0, keepdims=True)
            attended = (oacc[...] * inverse).astype(jnp.bfloat16).astype(jnp.float32)
            delta = jnp.sum(gt.astype(jnp.float32) * attended, axis=0, keepdims=True)
            qacc[...] = jnp.zeros_like(qacc)

            def grad_step(j, parts, _):
                last = (((1,), (1,)), ((), ()))

                def product(n):
                    return jnp.dot(vn[rows_of(j, n), :], gt, preferred_element_type=jnp.float32)

                prob, held, out = product(0), None, None
                for n in range(parts + 1):
                    later = product(n + 1) if n + 1 < parts else None
                    if n < parts:
                        shares = score[slot_of(j, n), :] * inverse
                        weights = shares.astype(jnp.bfloat16)
                        grad = (shares * (prob - delta)).astype(jnp.bfloat16)
                    if n:
                        old_weights, old_grad = held
                        m = j * ck + (n - 1) * SUB
                        kt = wide(kvt, m, pl.ds(0, HD), SUB)
                        term = jnp.dot(kt, old_grad, preferred_element_type=jnp.float32)
                        out = term if out is None else out + term
                        dk = lax.dot_general(qt, old_grad, last, preferred_element_type=jnp.float32)
                        dv = lax.dot_general(gt, old_weights, last, preferred_element_type=jnp.float32)
                        for c in range(SUB):
                            cols = slice(c * CH, (c + 1) * CH)
                            acc[m + c, :HD, :] += dk[:, cols]
                            acc[m + c, HD:, :] += dv[:, cols]
                    held = (weights, grad)
                    prob = later
                qacc[...] += out
                return 0

            sweep(grad_step, 0)
            out = (qacc[...] * FACTOR).astype(jnp.bfloat16)
            for n in range(cq):
                dq[n] = out[:, n * CH : (n + 1) * CH]
                done = acc[nc + i * cq + n]
                mine[n, :HD, :] = done[:HD] * FACTOR
                mine[n, HD:, :] = done[HD:]

        for count in range(1, (nc * CH + tq - 1) // tk + 2):
            pl.when(k_last - k_first == count)(functools.partial(run, count))

    q_step(nc // cq - 1 - step)

    @pl.when(step == nc // cq - 1)
    def _():
        def finish(c, _):
            back[c, :HD, :] = (acc[c, :HD, :] * FACTOR).astype(jnp.bfloat16)
            back[c, HD:, :] = acc[c, HD:, :].astype(jnp.bfloat16)
            return 0

        lax.fori_loop(0, nc, finish, 0, unroll=2)


def attend(lens, base, halo, own, qd, q_row, into=None, cq=2, ck=2):
    nc = halo.shape[0]
    tq, tk = cq * CH, ck * CH
    window = nc * CH + tq + tk
    spec = (nc, lens.shape[0], cq, ck, q_row)
    smem = pl.BlockSpec(memory_space=pltpu.SMEM)

    steps = nc // cq

    def whole(x):
        return pl.BlockSpec(x.shape, lambda i: (0, 0, 0))

    def part(rows):
        return pl.BlockSpec((cq, rows, CH), lambda i: (steps - 1 - i, 0, 0))

    through, extra, target, slot = [], (), (nc, HD, CH), 0
    if into is not None:
        through, extra, target = [pl.BlockSpec(memory_space=pl.ANY)], (into,), into.shape
        slot = into.shape[1] // HD - 1
    return pl.pallas_call(
        functools.partial(attend_kernel, spec),
        grid=(nc // cq,),
        out_shape=(
            pltpu.HBM(target, jnp.bfloat16),
            jax.ShapeDtypeStruct((nc, 2 * HD, CH), jnp.bfloat16),
            pltpu.HBM((nc, 2 * HD, CH), jnp.float32),
        ),
        in_specs=[smem, smem, whole(halo), whole(own), whole(qd)] + through,
        input_output_aliases={5: 0} if extra else {},
        out_specs=(
            pl.BlockSpec((cq, HD, CH), lambda i: (steps - 1 - i, slot, 0)),
            pl.BlockSpec((nc, 2 * HD, CH), lambda i: (0, 0, 0)),
            part(2 * HD),
        ),
        scratch_shapes=[
            pltpu.VMEM((2 * nc, 2 * HD, CH), jnp.bfloat16),
            pltpu.VMEM((2 * nc * CH, HD), jnp.bfloat16),
            pltpu.VMEM((2 * nc * CH, HD), jnp.bfloat16),
            pltpu.VMEM((window, tq), jnp.float32),
            pltpu.VMEM((2 * nc, 2 * HD, CH), jnp.float32),
            pltpu.VMEM((HD, tq), jnp.float32),
            pltpu.VMEM((HD, tq), jnp.float32),
        ],
        compiler_params=pltpu.CompilerParams(vmem_limit_bytes=ATTEND_VMEM),
        name="attend",
    )(lens, base, halo, own, qd, *extra)


def pack_kernel(plan, *refs):
    ins, outs = refs[: len(plan)], refs[len(plan) :]
    for source, (which, row) in zip(ins, plan):
        for m in range(source.shape[1] // (4 * HD)):
            block = source[:, m * 4 * HD : (m + 1) * 4 * HD].T
            for n in range(4):
                outs[which][4 * m + n, row : row + HD, :] = block[n * HD : (n + 1) * HD]


def pack(arrays, halves, plan, rows):
    tokens, columns = arrays[0].shape
    peers = columns // (2 * HD)
    return pl.pallas_call(
        functools.partial(pack_kernel, plan),
        grid=(1,),
        out_shape=tuple(jax.ShapeDtypeStruct((peers, r, tokens), jnp.bfloat16) for r in rows),
        in_specs=[pl.BlockSpec((tokens, columns // 2), lambda i, h=h: (0, h)) for h in halves],
        out_specs=tuple(pl.BlockSpec((peers, r, tokens), lambda i: (0, 0, 0)) for r in rows),
        compiler_params=pltpu.CompilerParams(vmem_limit_bytes=PACK_VMEM),
        name="pack",
    )(*arrays)


def unpack_kernel(plan, n_in, n_pass, *refs):
    ins, outs = refs[:n_in], refs[n_in + n_pass :]
    for target, (which, row) in zip(outs, plan):
        for m in range(target.shape[1] // (4 * HD)):
            parts = [ins[which][4 * m + n, row : row + HD, :] for n in range(4)]
            target[:, m * 4 * HD : (m + 1) * 4 * HD] = jnp.concatenate(parts, axis=0).T


def unpack(received, half, plan, earlier=()):
    peers, _, tokens = received[0].shape
    columns = 2 * peers * HD
    shape = jax.ShapeDtypeStruct((tokens, columns), jnp.bfloat16)
    n_in, n_pass = len(received), len(earlier)
    return pl.pallas_call(
        functools.partial(unpack_kernel, plan, n_in, n_pass),
        grid=(1,),
        out_shape=(shape,) * len(plan),
        in_specs=[pl.BlockSpec(r.shape, lambda i: (0, 0, 0)) for r in received]
        + [pl.BlockSpec(memory_space=pl.ANY)] * n_pass,
        out_specs=(pl.BlockSpec((tokens, columns // 2), lambda i: (0, half)),) * len(plan),
        input_output_aliases={n_in + n: n for n in range(n_pass)},
        compiler_params=pltpu.CompilerParams(vmem_limit_bytes=32 * 1024 * 1024),
        name="unpack",
    )(*received, *earlier)


def total_kernel(extra, *refs):
    mine, got, out = refs[extra], refs[extra + 1], refs[-1]
    if extra:
        out[:, :HD, :] = refs[0][...]
    base = HD if extra else 0
    out[:, base:, :] = (mine[...] + got[...].astype(jnp.float32)).astype(jnp.bfloat16)


def total(first, mine, got):
    peers, rows, tokens = mine.shape
    extra = len(first)
    steps = 2

    def part(height):
        return pl.BlockSpec((peers // steps, height, tokens), lambda i: (i, 0, 0))

    return pl.pallas_call(
        functools.partial(total_kernel, extra),
        grid=(steps,),
        out_shape=jax.ShapeDtypeStruct((peers, rows + HD * extra, tokens), jnp.bfloat16),
        in_specs=[part(HD)] * extra + [part(rows)] * 2,
        out_specs=part(rows + HD * extra),
        compiler_params=pltpu.CompilerParams(vmem_limit_bytes=TOTAL_VMEM),
        name="total",
    )(*first, mine, got)


def shards(queries, keys_in, values, out_grad, doc_lengths):
    blocks, group = lax.axis_size("blk"), lax.axis_size("head") // 2
    tokens = queries.shape[0]
    devices = 2 * blocks * group
    halves = [list(range(group)), list(range(group, 2 * group))]
    up = [(i, i + group) for i in range(devices - group)]
    down = [(i + group, i) for i in range(devices - group)]

    def exchange(x):
        return lax.all_to_all(
            x, "head", split_axis=0, concat_axis=0, tiled=True, axis_index_groups=halves
        )

    def shift(x, route):
        return lax.ppermute(x, ("blk", "head"), route)

    def after(x, *earlier):
        return lax.optimization_barrier((x, *earlier))[0]

    half_index = lax.axis_index("blk") * 2 + lax.axis_index("head") // group
    base = (half_index * (group * tokens)).astype(jnp.int32).reshape(1)
    pair = ((0, 0), (0, HD))

    def pack_pair(first, second, half):
        return pack((first, second), (half, half), pair, (2 * HD,))[0]

    send_kv_a = pack_pair(keys_in, values, 0)
    send_q_b = pack_pair(queries, out_grad, 1)
    four = ((0, 0), (0, HD), (0, 2 * HD), (0, 3 * HD))
    (send_mid,) = pack((queries, out_grad, keys_in, values), (0, 0, 1, 1), four, (4 * HD,))

    own_a = exchange(send_kv_a)
    halo_a = shift(own_a, up)
    middle = exchange(after(send_mid, own_a, send_q_b))
    own_b = middle[:, 2 * HD :, :]
    halo_b = shift(own_b, up)
    rows_b = exchange(after(send_q_b, middle, halo_a))
    dq_a, back_a, mine_a = attend(doc_lengths, base, halo_a, own_a, middle, 0)
    got_a = shift(back_a, down)
    out_q = exchange(after(dq_a, rows_b, halo_b))
    dq_b, back_b, mine_b = attend(doc_lengths, base, halo_b, own_b, rows_b, 0)
    got_b = shift(back_b, down)
    sum_a = total((dq_b,), mine_a, got_a)
    out_a = exchange(after(sum_a, out_q))
    sum_b = total((), mine_b, got_b)
    out_b = exchange(after(sum_b, out_a))
    grad_q, grad_k, grad_v = unpack((out_q, out_a), 0, ((0, 0), (1, HD), (1, 2 * HD)))
    (grad_q,) = unpack((out_a,), 1, ((0, 0),), (grad_q,))
    grad_k, grad_v = unpack((out_b,), 1, pair, (grad_k, grad_v))
    return grad_q, grad_k, grad_v


def solution(mesh):
    rows = P(("blk", "head"), None)
    return jax.shard_map(
        shards,
        mesh=mesh,
        in_specs=(rows, rows, rows, rows, P()),
        out_specs=(rows, rows, rows),
        check_vma=False,
    )
```
